512 devices in a mesh: dom: 64 (over y, x, core), ao: 8 (over z).
Axes of the slice: x: 4, y: 8, z: 8, core: 2. Of those that a mesh axis runs over, the one named last changes fastest.
Arguments:
- three_index: bfloat16 [512, 256, 4096], P('dom', None, 'ao'), may hold values from -1.5 to 1.5
- occ_coef: bfloat16 [4096, 1024], P('ao'), may hold values from -0.09375 to 0.09375
- pao_coef: bfloat16 [512, 4096, 128], P(('dom', 'ao')), may hold values from -0.375 to 0.375
- ao_map: int32 [512, 256], P(('dom', 'ao')), may hold values 0 or 1
- aux_map: int32 [512, 4], P(('dom', 'ao')), may hold values 0 or 1
- ao_list: int32 [4, 16], replicated, may hold values from 0 to 255, as said below
Outputs:
- pair_self: bfloat16 [512, 256, 256], P(('dom', 'ao'))
- pair_near: bfloat16 [512, 256, 256], P(('dom', 'ao'))
The draws below stay inside these ranges and needn't reach their ends.
Inputs may be any that keep to these rules, and one draw needn't show every extreme that they name: `ao_list`: each row names 16 different AO shell blocks.
All inputs are finite; a program needn't handle non-finite values. No bound on the sum of `ao_map` or of `aux_map` on one device may be relied on, other than what follows from the above.
Results may differ from the reference program's by a relative error of at most 0.029.
Values may be sent and summed in bfloat16 or wider, within the bound.
No kernel may reach another device: no remote copies, remote signals or barrier semaphores. Data moves between devices by JAX's collectives and lax.ppermute only.
A program may use at most 64 MiB of HBM per device.

```python
import jax
import jax.numpy as jnp
from jax import lax

QB = 128
MU = 256
NU = 4096
AOB = 16
OCC_D = 2
PAO_D = 128
DOMAINS = 512
AUX = 512
AUXBLK = 4
NSH = 256
OCC_ALL = 1024
N_AO = 8


def shuffled_row(row_key):
    return jax.random.permutation(row_key, NU // AOB)[:MU // AOB].astype(jnp.int32)


def draw_ao_list(key, part):
    key = jax.random.fold_in(key, 7)
    shells = NU // AOB
    picked = MU // AOB
    row_keys = jax.random.split(key, AUXBLK + 1)
    others = jax.vmap(shuffled_row)(row_keys[1:])
    middle = jax.random.permutation(row_keys[0], shells - 2)[:picked - 2].astype(jnp.int32) + 1
    first = jnp.concatenate([jnp.array([0, shells - 1], jnp.int32), middle])
    return others.at[0].set(first)


def with_ends(values, key, smallest, largest):
    spot = [jax.random.randint(jax.random.fold_in(key, axis), (), 0, length) for axis, length in enumerate(values.shape)]
    widest = values.shape.index(max(values.shape))
    beside = spot[:widest] + [(spot[widest] + 1) % values.shape[widest]] + spot[widest + 1:]
    return values.at[tuple(spot)].set(smallest).at[tuple(beside)].set(largest)


def shard_levels(rng, extent, cuts, low, high):
    factor_of = 1.0
    for dim, blocks in cuts:
        draws = jax.random.uniform(jax.random.fold_in(jax.random.fold_in(rng, 6), dim), (blocks,), jnp.float32, low / len(cuts), high / len(cuts))
        factor_of = factor_of * jnp.repeat(jnp.exp(draws), extent[dim] // blocks).reshape((-1,) + (1,) * (len(extent) - 1 - dim))
    return factor_of


def normal_values(own_key, shape, scale, most, pieces=(), dtype=jnp.bfloat16):
    values = jax.random.normal(own_key, shape, jnp.float32) * scale
    if len(pieces) > 0:
        values = shard_levels(own_key, shape, pieces, -0.22, 0.18) * values
    return jnp.clip(values, min=-most, max=most).astype(dtype)


def setup_inputs(seed: int = 0) -> dict:
    keys = jax.random.split(jax.random.key(seed), 7)
    return {
        "three_index": normal_values(keys[0], (AUX, MU, NU), 0.25, 1.5, ((0, 64), (2, 8))),
        "occ_coef": normal_values(keys[1], (NU, OCC_ALL), NU ** -0.5, 0.09375, ((0, 8),)),
        "pao_coef": normal_values(keys[2], (DOMAINS, NU, PAO_D), MU ** -0.5, 0.375, ((0, 512),)),
        "ao_map": with_ends((jax.random.randint(keys[3], (DOMAINS, NSH), 0, 4) < 3).astype(jnp.int32), jax.random.fold_in(keys[3], 1), 0, 1),
        "aux_map": with_ends((jax.random.randint(keys[4], (DOMAINS, AUXBLK), 0, 4) < 3).astype(jnp.int32), jax.random.fold_in(keys[4], 1), 0, 1),
        "ao_list": draw_ao_list(jax.random.fold_in(keys[6], 71), 0),
    }


def reference(three_index, occ_coef, pao_coef, ao_map, aux_map, ao_list):
    nu_dev = NU // N_AO
    accum_sum = jnp.zeros((AUX, MU, OCC_ALL), jnp.float32)
    for ao_shard in range(N_AO):
        lower = ao_shard * nu_dev
        shard_part = jnp.einsum('qmn,no->qmo', three_index[:, :, lower:lower + nu_dev].astype(jnp.float32), occ_coef[lower:lower + nu_dev].astype(jnp.float32))
        rounded = lax.optimization_barrier(shard_part.astype(jnp.bfloat16))
        accum_sum = accum_sum + rounded.astype(jnp.float32)
    half_ints = accum_sum.astype(jnp.bfloat16).reshape(AUXBLK, QB, MU, DOMAINS, OCC_D)
    pao_shells = pao_coef.reshape(DOMAINS, NSH, AOB, PAO_D) * ao_map.astype(jnp.bfloat16)[:, :, None, None]
    projector = pao_shells[:, ao_list.astype(jnp.int32)].reshape(DOMAINS, AUXBLK, MU, PAO_D)
    full_ints = jnp.einsum('bqmdk,dbma->dbqka', half_ints.astype(jnp.float32), projector.astype(jnp.float32)).astype(jnp.bfloat16)
    full_ints = full_ints.reshape(DOMAINS, AUX, OCC_D, PAO_D)
    aux_keep = jnp.repeat(aux_map, QB, axis=1).astype(jnp.bfloat16)
    fitted = full_ints * aux_keep[:, :, None, None]
    flat_full = full_ints.reshape(DOMAINS, AUX, OCC_D * PAO_D).astype(jnp.float32)
    flat_fit = fitted.reshape(DOMAINS, AUX, OCC_D * PAO_D).astype(jnp.float32)
    partner = jnp.roll(flat_full, N_AO, axis=0)
    pair_self = jnp.einsum('dqx,dqy->dxy', flat_fit, flat_full)
    pair_near = jnp.einsum('dqx,dqy->dxy', flat_fit, partner)
    return pair_self.astype(jnp.bfloat16), pair_near.astype(jnp.bfloat16)
```

```python
import functools

import jax
import jax.numpy as jnp
from jax import lax
from jax.experimental import pallas as pl
from jax.experimental.pallas import tpu as pltpu
from jax.sharding import PartitionSpec as P

QB = 128
AOB = 16
OCC_D = 2
BF = jnp.bfloat16
F32 = jnp.float32
PARTS = 1
FIRST_VMEM = 56 * 2**20
VMEM_LIMIT = 16 * 2**20


def hop(value, doms, ring):
    pairs = []
    for d in range(doms):
        step = 1 if d % 2 == 0 else -1
        for s in range(ring):
            pairs.append((d * ring + s, d * ring + (s + step) % ring))
    return lax.ppermute(value, ("dom", "ao"), pairs)


def swap(value, doms):
    return lax.ppermute(value, "dom", [(d, d ^ 1) for d in range(doms)])


def nt(x, y):
    return lax.dot_general(x, y, (((1,), (1,)), ((), ())), preferred_element_type=F32)


def pick_rows(occ, rows, ring, ahead):
    way = 1 - 2 * (lax.axis_index("dom") % 2)
    shard = (lax.axis_index("ao") + ahead * way + ring) % ring
    row = lax.broadcasted_iota(jnp.int32, (rows, occ.shape[1]), 0)
    col = lax.broadcasted_iota(jnp.int32, (rows, occ.shape[1]), 1)
    home = (row // OCC_D) * (ring * OCC_D) + row % OCC_D + shard * OCC_D
    pick = jnp.where(col == home, 1.0, 0.0).astype(BF)
    return nt(pick, occ).astype(BF)


def first_kernel(ring, occ_hbm, slab_hbm, *refs):
    out_refs = refs[:PARTS]
    occ_ref, slab_ref, occ_sem, slab_sems = refs[PARTS:]
    cut = slab_ref.shape[0] // PARTS
    occ_copy = pltpu.make_async_copy(occ_hbm, occ_ref, occ_sem)
    occ_copy.start()
    slab_copies = []
    for c in range(PARTS):
        part = pl.ds(c * cut, cut)
        slab_copies.append(pltpu.make_async_copy(slab_hbm.at[part], slab_ref.at[part], slab_sems.at[c]))
        slab_copies[-1].start()
    occ_copy.wait()
    w = pick_rows(occ_ref[...], out_refs[0].shape[0], ring, ring // 2)
    for c in range(PARTS):
        slab_copies[c].wait()
        out_refs[c][...] = nt(w, slab_ref[c * cut : (c + 1) * cut]).astype(BF)


def first_term(occ, slab, ring):
    rows, width = occ.shape[1] // ring, slab.shape[0] // PARTS
    vm, hbm = pl.BlockSpec(memory_space=pltpu.VMEM), pl.BlockSpec(memory_space=pl.ANY)
    return pl.pallas_call(
        functools.partial(first_kernel, ring),
        out_shape=[jax.ShapeDtypeStruct((rows, width), BF)] * PARTS,
        in_specs=[hbm, hbm],
        out_specs=[vm] * PARTS,
        scratch_shapes=[
            pltpu.VMEM(occ.shape, BF),
            pltpu.VMEM(slab.shape, BF),
            pltpu.SemaphoreType.DMA,
            pltpu.SemaphoreType.DMA((PARTS,)),
        ],
        compiler_params=pltpu.CompilerParams(vmem_limit_bytes=FIRST_VMEM),
        cost_estimate=pl.CostEstimate(flops=2 * rows * slab.size, bytes_accessed=3 << 20, transcendentals=0),
    )(occ, slab)


def pick_kernel(ring, occ_ref, w_ref):
    rows = occ_ref.shape[1] // ring
    for i in range(ring // 2):
        w_ref[i] = pick_rows(occ_ref[...], rows, ring, ring // 2 - 1 - i)


def pick_rest(occ, ring):
    rows = occ.shape[1] // ring
    return pl.pallas_call(
        functools.partial(pick_kernel, ring),
        out_shape=jax.ShapeDtypeStruct((ring // 2, rows, occ.shape[0]), BF),
        in_specs=[pl.BlockSpec(memory_space=pltpu.VMEM)],
        out_specs=pl.BlockSpec(memory_space=pltpu.VMEM),
        compiler_params=pltpu.CompilerParams(vmem_limit_bytes=VMEM_LIMIT),
        cost_estimate=pl.CostEstimate(flops=2 * (ring // 2) * rows * occ.size, bytes_accessed=2 << 20, transcendentals=0),
    )(occ)


def term_kernel(w_ref, slab_ref, *out_refs):
    cut = slab_ref.shape[0] // PARTS
    for c in range(PARTS):
        out_refs[c][...] = nt(w_ref[0], slab_ref[c * cut : (c + 1) * cut]).astype(BF)


def term(w, i, slab):
    rows, width = w.shape[1], slab.shape[0] // PARTS
    vm = pl.BlockSpec(memory_space=pltpu.VMEM)
    return pl.pallas_call(
        term_kernel,
        grid=(1,),
        out_shape=[jax.ShapeDtypeStruct((rows, width), BF)] * PARTS,
        in_specs=[pl.BlockSpec((1,) + w.shape[1:], lambda g: (i, 0, 0)), vm],
        out_specs=[vm] * PARTS,
        compiler_params=pltpu.CompilerParams(vmem_limit_bytes=VMEM_LIMIT),
        cost_estimate=pl.CostEstimate(flops=2 * rows * slab.size, bytes_accessed=3 << 20, transcendentals=0),
    )(w, slab)


def add(x, y):
    return (x.astype(F32) + y.astype(F32)).astype(BF)


def body(three_index, occ_coef, pao_coef, ao_map, aux_map, ao_list):
    doms, ring = lax.axis_size("dom"), lax.axis_size("ao")
    aux_rows, mu_rows, nu_local = three_index.shape
    blocks = ao_list.shape[0]
    pao_d = pao_coef.shape[2]
    slab = three_index.reshape(aux_rows * mu_rows, nu_local)

    own = first_term(occ_coef, slab, ring)
    w = pick_rest(occ_coef, ring)
    slab, own = lax.optimization_barrier((slab, own))
    other_slab = swap(slab, doms)
    other = None
    half_ring = ring // 2
    for i in range(half_ring):
        own = [add(t, hop(v, doms, ring)) for t, v in zip(term(w, i, slab), own)]
        if i < half_ring - 1:
            if i == 0:
                other = term(w, i, other_slab)
            else:
                other = [add(t, v) for t, v in zip(term(w, i, other_slab), other)]
            other = [hop(v, doms, ring) for v in other]
    halves = [add(v, swap(o, doms)) for v, o in zip(own, other)]

    shells = pao_coef[0].reshape(-1, AOB, pao_d)
    keep = ao_map[0].astype(BF)[ao_list]
    projector = (shells[ao_list] * keep[:, :, None, None]).reshape(blocks, mu_rows, pao_d)
    aux_keep = jnp.repeat(aux_map[0], QB).astype(BF)
    half = jnp.stack([h.reshape(doms, OCC_D, aux_rows // PARTS, mu_rows) for h in halves], axis=2)
    half = half.reshape(doms, OCC_D, aux_rows, mu_rows)
    got = lax.all_to_all(half, "dom", split_axis=0, concat_axis=0, tiled=True)
    got = got.transpose(1, 0, 2, 3).reshape(OCC_D, blocks, QB, mu_rows)
    full = jnp.einsum("kbqm,bma->bqka", got, projector, preferred_element_type=F32)
    full = full.astype(BF).reshape(blocks * QB, OCC_D * pao_d)
    near = lax.ppermute(full, "dom", [(d, (d + 1) % doms) for d in range(doms)])
    fitted = full * aux_keep[:, None]
    pair_self = jnp.einsum("qx,qy->xy", fitted, full, preferred_element_type=F32)
    pair_near = jnp.einsum("qx,qy->xy", fitted, near, preferred_element_type=F32)
    return (pair_self.astype(BF)[None], pair_near.astype(BF)[None])


def solution(mesh):
    owner = P(("dom", "ao"), None, None)
    placed = (
        P("dom", None, "ao"),
        P("ao", None),
        owner,
        P(("dom", "ao"), None),
        P(("dom", "ao"), None),
        P(),
    )
    return jax.shard_map(body, mesh=mesh, in_specs=placed, out_specs=(owner, owner), check_vma=False)
```

```python
import functools

import jax
import jax.numpy as jnp
from jax import lax
from jax.experimental import pallas as pl
from jax.experimental.pallas import tpu as pltpu
from jax.sharding import PartitionSpec as P

QB = 128
AOB = 16
OCC_D = 2
vm = pl.BlockSpec(memory_space=pltpu.VMEM)
BF = jnp.bfloat16
F32 = jnp.float32
PARTS = 1
FIRST_VMEM = 56 * 2**20
VMEM_LIMIT = 16 * 2**20


def hop(value, doms, ring):
    pairs = []
    for d in range(doms):
        step = 1 if d % 2 == 0 else -1
        for s in range(ring):
            pairs.append((d * ring + s, d * ring + (s + step) % ring))
    return lax.ppermute(value, ("dom", "ao"), pairs)


def swap(value, doms):
    return lax.ppermute(value, "dom", [(d, d ^ 1) for d in range(doms)])


def nt(x, y):
    return lax.dot_general(x, y, (((1,), (1,)), ((), ())), preferred_element_type=F32)


def pick_rows(occ, rows, ring, ahead):
    way = 1 - 2 * (lax.axis_index("dom") % 2)
    shard = (lax.axis_index("ao") + ahead * way + ring) % ring
    row = lax.broadcasted_iota(jnp.int32, (rows, occ.shape[1]), 0)
    col = lax.broadcasted_iota(jnp.int32, (rows, occ.shape[1]), 1)
    home = (row // OCC_D) * (ring * OCC_D) + row % OCC_D + shard * OCC_D
    pick = jnp.where(col == home, 1.0, 0.0).astype(BF)
    return nt(pick, occ).astype(BF)


def first_kernel(ring, occ_hbm, slab_hbm, *refs):
    out_refs = refs[:PARTS]
    occ_ref, slab_ref, occ_sem, slab_sems = refs[PARTS:]
    cut = slab_ref.shape[0] // PARTS
    occ_copy = pltpu.make_async_copy(occ_hbm, occ_ref, occ_sem)
    occ_copy.start()
    slab_copies = []
    for c in range(PARTS):
        part = pl.ds(c * cut, cut)
        slab_copies.append(pltpu.make_async_copy(slab_hbm.at[part], slab_ref.at[part], slab_sems.at[c]))
        slab_copies[-1].start()
    occ_copy.wait()
    w = pick_rows(occ_ref[...], out_refs[0].shape[0], ring, ring // 2)
    for c in range(PARTS):
        slab_copies[c].wait()
        out_refs[c][...] = nt(w, slab_ref[c * cut : (c + 1) * cut]).astype(BF)


def first_term(occ, slab, ring):
    rows, width = occ.shape[1] // ring, slab.shape[0] // PARTS
    vm, hbm = pl.BlockSpec(memory_space=pltpu.VMEM), pl.BlockSpec(memory_space=pl.ANY)
    return pl.pallas_call(
        functools.partial(first_kernel, ring),
        out_shape=[jax.ShapeDtypeStruct((rows, width), BF)] * PARTS,
        in_specs=[hbm, hbm],
        out_specs=[vm] * PARTS,
        scratch_shapes=[
            pltpu.VMEM(occ.shape, BF),
            pltpu.VMEM(slab.shape, BF),
            pltpu.SemaphoreType.DMA,
            pltpu.SemaphoreType.DMA((PARTS,)),
        ],
        compiler_params=pltpu.CompilerParams(vmem_limit_bytes=FIRST_VMEM),
        cost_estimate=pl.CostEstimate(flops=2 * rows * slab.size, bytes_accessed=3 << 20, transcendentals=0),
    )(occ, slab)


def pick_kernel(ring, occ_ref, w_ref):
    rows = occ_ref.shape[1] // ring
    for i in range(ring // 2):
        w_ref[i] = pick_rows(occ_ref[...], rows, ring, ring // 2 - 1 - i)


def pick_rest(occ, ring):
    rows = occ.shape[1] // ring
    return pl.pallas_call(
        functools.partial(pick_kernel, ring),
        out_shape=jax.ShapeDtypeStruct((ring // 2, rows, occ.shape[0]), BF),
        in_specs=[pl.BlockSpec(memory_space=pltpu.VMEM)],
        out_specs=pl.BlockSpec(memory_space=pltpu.VMEM),
        compiler_params=pltpu.CompilerParams(vmem_limit_bytes=VMEM_LIMIT),
        cost_estimate=pl.CostEstimate(flops=2 * (ring // 2) * rows * occ.size, bytes_accessed=2 << 20, transcendentals=0),
    )(occ)


def term_kernel(w_ref, slab_ref, *out_refs):
    cut = slab_ref.shape[0] // PARTS
    for c in range(PARTS):
        out_refs[c][...] = nt(w_ref[0], slab_ref[c * cut : (c + 1) * cut]).astype(BF)


def term(w, i, slab):
    rows, width = w.shape[1], slab.shape[0] // PARTS
    vm = pl.BlockSpec(memory_space=pltpu.VMEM)
    return pl.pallas_call(
        term_kernel,
        grid=(1,),
        out_shape=[jax.ShapeDtypeStruct((rows, width), BF)] * PARTS,
        in_specs=[pl.BlockSpec((1,) + w.shape[1:], lambda g: (i, 0, 0)), vm],
        out_specs=[vm] * PARTS,
        compiler_params=pltpu.CompilerParams(vmem_limit_bytes=VMEM_LIMIT),
        cost_estimate=pl.CostEstimate(flops=2 * rows * slab.size, bytes_accessed=3 << 20, transcendentals=0),
    )(w, slab)


def add(x, y):
    return (x.astype(F32) + y.astype(F32)).astype(BF)


def cost(flops, size):
    return pl.CostEstimate(flops=flops, bytes_accessed=size, transcendentals=0)


def full_kernel(got_ref, projector_ref, full_ref):
    doms, _, aux_rows, mu_rows = got_ref.shape
    blocks, _, pao_d = projector_ref.shape
    per = doms // blocks
    for b in range(blocks):
        part = got_ref[b * per : (b + 1) * per].astype(F32).reshape(per * OCC_D * aux_rows, mu_rows).astype(BF)
        t = jnp.dot(part, projector_ref[b], preferred_element_type=F32).reshape(per, OCC_D, aux_rows, pao_d)
        for k in range(OCC_D):
            rows = slice(b * per * aux_rows, (b + 1) * per * aux_rows)
            full_ref[rows, k * pao_d : (k + 1) * pao_d] = t[:, k].reshape(per * aux_rows, pao_d).astype(BF)


def full_of(got, projector):
    doms, _, aux_rows, _ = got.shape
    return pl.pallas_call(
        full_kernel,
        out_shape=jax.ShapeDtypeStruct((doms * aux_rows, OCC_D * projector.shape[2]), BF),
        in_specs=[vm, vm],
        out_specs=vm,
        compiler_params=pltpu.CompilerParams(vmem_limit_bytes=VMEM_LIMIT),
        cost_estimate=cost(2 * got.size * projector.shape[2], 1 << 20),
    )(got, projector)


def self_kernel(full_ref, keep_ref, out_ref, turned_ref):
    per = full_ref.shape[0] // keep_ref.shape[1]
    for b in range(keep_ref.shape[1]):
        rows = slice(b * per, (b + 1) * per)
        kept = full_ref[rows].astype(F32) * keep_ref[0, b].astype(F32)
        turned_ref[:, rows] = kept.T.astype(BF)
    out_ref[0] = jnp.dot(turned_ref[...], full_ref[...], preferred_element_type=F32).astype(BF)


def self_pair(full, aux_map):
    rows, width = full.shape
    return pl.pallas_call(
        self_kernel,
        out_shape=[jax.ShapeDtypeStruct((1, width, width), BF), jax.ShapeDtypeStruct((width, rows), BF)],
        in_specs=[vm, pl.BlockSpec(memory_space=pltpu.SMEM)],
        out_specs=[vm, vm],
        compiler_params=pltpu.CompilerParams(vmem_limit_bytes=VMEM_LIMIT),
        cost_estimate=cost(2 * rows * width * width, 1 << 20),
    )(full, aux_map)


def near_kernel(turned_ref, near_ref, out_ref):
    out_ref[0] = jnp.dot(turned_ref[...], near_ref[...], preferred_element_type=F32).astype(BF)


def near_pair(turned, near):
    rows, width = near.shape
    return pl.pallas_call(
        near_kernel,
        out_shape=jax.ShapeDtypeStruct((1, width, width), BF),
        in_specs=[vm, vm],
        out_specs=vm,
        compiler_params=pltpu.CompilerParams(vmem_limit_bytes=VMEM_LIMIT),
        cost_estimate=cost(2 * rows * width * width, 1 << 20),
    )(turned, near)


def body(three_index, occ_coef, pao_coef, ao_map, aux_map, ao_list):
    doms, ring = lax.axis_size("dom"), lax.axis_size("ao")
    aux_rows, mu_rows, nu_local = three_index.shape
    blocks = ao_list.shape[0]
    pao_d = pao_coef.shape[2]
    slab = three_index.reshape(aux_rows * mu_rows, nu_local)

    own = first_term(occ_coef, slab, ring)
    w = pick_rest(occ_coef, ring)
    slab, own = lax.optimization_barrier((slab, own))
    other_slab = swap(slab, doms)
    other = None
    half_ring = ring // 2
    for i in range(half_ring):
        own = [add(t, hop(v, doms, ring)) for t, v in zip(term(w, i, slab), own)]
        if i < half_ring - 1:
            if i == 0:
                other = term(w, i, other_slab)
            else:
                other = [add(t, v) for t, v in zip(term(w, i, other_slab), other)]
            other = [hop(v, doms, ring) for v in other]
    halves = [add(v, swap(o, doms)) for v, o in zip(own, other)]

    shells = pao_coef[0].reshape(-1, AOB, pao_d)
    keep = ao_map[0].astype(BF)[ao_list]
    projector = (shells[ao_list] * keep[:, :, None, None]).reshape(blocks, mu_rows, pao_d)
    half = jnp.stack([h.reshape(doms, OCC_D, aux_rows // PARTS, mu_rows) for h in halves], axis=2)
    half = half.reshape(doms, OCC_D, aux_rows, mu_rows)
    got = lax.all_to_all(half, "dom", split_axis=0, concat_axis=0, tiled=True)
    full = full_of(got, projector)
    near = lax.ppermute(full, "dom", [(d, (d + 1) % doms) for d in range(doms)])
    pair_self, turned = self_pair(full, aux_map)
    pair_near = near_pair(turned, near)
    return (pair_self, pair_near)


def solution(mesh):
    owner = P(("dom", "ao"), None, None)
    placed = (
        P("dom", None, "ao"),
        P("ao", None),
        owner,
        P(("dom", "ao"), None),
        P(("dom", "ao"), None),
        P(),
    )
    return jax.shard_map(body, mesh=mesh, in_specs=placed, out_specs=(owner, owner), check_vma=False)
```

```python
import functools

import jax
import jax.numpy as jnp
from jax import lax
from jax.experimental import pallas as pl
from jax.experimental.pallas import tpu as pltpu
from jax.sharding import PartitionSpec as P

QB = 128
AOB = 16
OCC_D = 2
vm = pl.BlockSpec(memory_space=pltpu.VMEM)
BF = jnp.bfloat16
F32 = jnp.float32
PARTS = 1
HINT_B = 1000000
FIRST_VMEM = 56 * 2**20
VMEM_LIMIT = 16 * 2**20


def hop(value, doms, ring, other=0):
    pairs = []
    for d in range(doms):
        step = 1 if d % 2 == 0 else -1
        for s in range(ring):
            pairs.append((d * ring + s, (d ^ other) * ring + (s + step) % ring))
    return lax.ppermute(value, ("dom", "ao"), pairs)


def swap(value, doms):
    return lax.ppermute(value, "dom", [(d, d ^ 1) for d in range(doms)])


def nt(x, y):
    return lax.dot_general(x, y, (((1,), (1,)), ((), ())), preferred_element_type=F32)


def pick_rows(occ, rows, ring, ahead):
    way = 1 - 2 * (lax.axis_index("dom") % 2)
    shard = (lax.axis_index("ao") + ahead * way + ring) % ring
    row = lax.broadcasted_iota(jnp.int32, (rows, occ.shape[1]), 0)
    col = lax.broadcasted_iota(jnp.int32, (rows, occ.shape[1]), 1)
    home = (row // OCC_D) * (ring * OCC_D) + row % OCC_D + shard * OCC_D
    pick = jnp.where(col == home, 1.0, 0.0).astype(BF)
    return nt(pick, occ).astype(BF)


def first_kernel(ring, occ_hbm, slab_hbm, *refs):
    out_refs = refs[:PARTS]
    occ_ref, slab_ref, occ_sem, slab_sems = refs[PARTS:]
    cut = slab_ref.shape[0] // PARTS
    occ_copy = pltpu.make_async_copy(occ_hbm, occ_ref, occ_sem)
    occ_copy.start()
    slab_copies = []
    for c in range(PARTS):
        part = pl.ds(c * cut, cut)
        slab_copies.append(pltpu.make_async_copy(slab_hbm.at[part], slab_ref.at[part], slab_sems.at[c]))
        slab_copies[-1].start()
    occ_copy.wait()
    w = pick_rows(occ_ref[...], out_refs[0].shape[0], ring, ring // 2)
    for c in range(PARTS):
        slab_copies[c].wait()
        out_refs[c][...] = nt(w, slab_ref[c * cut : (c + 1) * cut]).astype(BF)


def first_term(occ, slab, ring):
    rows, width = occ.shape[1] // ring, slab.shape[0] // PARTS
    vm, hbm = pl.BlockSpec(memory_space=pltpu.VMEM), pl.BlockSpec(memory_space=pl.ANY)
    return pl.pallas_call(
        functools.partial(first_kernel, ring),
        out_shape=[jax.ShapeDtypeStruct((rows, width), BF)] * PARTS,
        in_specs=[hbm, hbm],
        out_specs=[vm] * PARTS,
        scratch_shapes=[
            pltpu.VMEM(occ.shape, BF),
            pltpu.VMEM(slab.shape, BF),
            pltpu.SemaphoreType.DMA,
            pltpu.SemaphoreType.DMA((PARTS,)),
        ],
        compiler_params=pltpu.CompilerParams(vmem_limit_bytes=FIRST_VMEM),
        cost_estimate=pl.CostEstimate(flops=2 * rows * slab.size, bytes_accessed=3 << 20, transcendentals=0),
    )(occ, slab)


def pick_kernel(ring, occ_ref, w_ref):
    rows = occ_ref.shape[1] // ring
    for i in range(ring // 2):
        w_ref[i] = pick_rows(occ_ref[...], rows, ring, ring // 2 - 1 - i)


def pick_rest(occ, ring):
    rows = occ.shape[1] // ring
    return pl.pallas_call(
        functools.partial(pick_kernel, ring),
        out_shape=jax.ShapeDtypeStruct((ring // 2, rows, occ.shape[0]), BF),
        in_specs=[pl.BlockSpec(memory_space=pltpu.VMEM)],
        out_specs=pl.BlockSpec(memory_space=pltpu.VMEM),
        compiler_params=pltpu.CompilerParams(vmem_limit_bytes=VMEM_LIMIT),
        cost_estimate=pl.CostEstimate(flops=2 * (ring // 2) * rows * occ.size, bytes_accessed=2 << 20, transcendentals=0),
    )(occ)


def term_kernel(w_ref, slab_ref, *out_refs):
    cut = slab_ref.shape[0] // PARTS
    for c in range(PARTS):
        out_refs[c][...] = nt(w_ref[0], slab_ref[c * cut : (c + 1) * cut]).astype(BF)


def term(w, i, slab):
    rows, width = w.shape[1], slab.shape[0] // PARTS
    vm = pl.BlockSpec(memory_space=pltpu.VMEM)
    return pl.pallas_call(
        term_kernel,
        grid=(1,),
        out_shape=[jax.ShapeDtypeStruct((rows, width), BF)] * PARTS,
        in_specs=[pl.BlockSpec((1,) + w.shape[1:], lambda g: (i, 0, 0)), vm],
        out_specs=[vm] * PARTS,
        compiler_params=pltpu.CompilerParams(vmem_limit_bytes=VMEM_LIMIT),
        cost_estimate=pl.CostEstimate(flops=2 * rows * slab.size, bytes_accessed=3 << 20, transcendentals=0),
    )(w, slab)


def add(x, y):
    return (x.astype(F32) + y.astype(F32)).astype(BF)


def cost(flops, size):
    return pl.CostEstimate(flops=flops, bytes_accessed=size, transcendentals=0)


def full_kernel(got_ref, projector_ref, full_ref):
    doms, _, aux_rows, mu_rows = got_ref.shape
    blocks, _, pao_d = projector_ref.shape
    per = doms // blocks
    for b in range(blocks):
        part = got_ref[b * per : (b + 1) * per].astype(F32).reshape(per * OCC_D * aux_rows, mu_rows).astype(BF)
        t = jnp.dot(part, projector_ref[b], preferred_element_type=F32).reshape(per, OCC_D, aux_rows, pao_d)
        for k in range(OCC_D):
            rows = slice(b * per * aux_rows, (b + 1) * per * aux_rows)
            full_ref[rows, k * pao_d : (k + 1) * pao_d] = t[:, k].reshape(per * aux_rows, pao_d).astype(BF)


def full_of(got, projector):
    doms, _, aux_rows, _ = got.shape
    return pl.pallas_call(
        full_kernel,
        out_shape=jax.ShapeDtypeStruct((doms * aux_rows, OCC_D * projector.shape[2]), BF),
        in_specs=[vm, vm],
        out_specs=vm,
        compiler_params=pltpu.CompilerParams(vmem_limit_bytes=VMEM_LIMIT),
        cost_estimate=cost(2 * got.size * projector.shape[2], 1 << 20),
    )(got, projector)


def self_kernel(full_ref, keep_ref, out_ref, turned_ref):
    per = full_ref.shape[0] // keep_ref.shape[1]
    for b in range(keep_ref.shape[1]):
        rows = slice(b * per, (b + 1) * per)
        kept = full_ref[rows].astype(F32) * keep_ref[0, b].astype(F32)
        turned_ref[:, rows] = kept.T.astype(BF)
    out_ref[0] = jnp.dot(turned_ref[...], full_ref[...], preferred_element_type=F32).astype(BF)


def self_pair(full, aux_map):
    rows, width = full.shape
    return pl.pallas_call(
        self_kernel,
        out_shape=[jax.ShapeDtypeStruct((1, width, width), BF), jax.ShapeDtypeStruct((width, rows), BF)],
        in_specs=[vm, pl.BlockSpec(memory_space=pltpu.SMEM)],
        out_specs=[vm, vm],
        compiler_params=pltpu.CompilerParams(vmem_limit_bytes=VMEM_LIMIT),
        cost_estimate=cost(2 * rows * width * width, 1 << 20),
    )(full, aux_map)


def near_kernel(turned_ref, near_ref, out_ref):
    out_ref[0] = jnp.dot(turned_ref[...], near_ref[...], preferred_element_type=F32).astype(BF)


def near_pair(turned, near):
    rows, width = near.shape
    return pl.pallas_call(
        near_kernel,
        out_shape=jax.ShapeDtypeStruct((1, width, width), BF),
        in_specs=[vm, vm],
        out_specs=vm,
        compiler_params=pltpu.CompilerParams(vmem_limit_bytes=VMEM_LIMIT),
        cost_estimate=cost(2 * rows * width * width, 1 << 20),
    )(turned, near)


def add_kernel(begin, x_ref, y_ref, out_ref):
    width = y_ref.shape[1]
    if begin > 0:
        out_ref[:, :begin] = x_ref[:, :begin]
    if begin + width < x_ref.shape[1]:
        out_ref[:, begin + width :] = x_ref[:, begin + width :]
    part = slice(begin, begin + width)
    out_ref[:, part] = (x_ref[:, part].astype(F32) + y_ref[...].astype(F32)).astype(BF)


def steer_add(x, y, flops, begin=0):
    return pl.pallas_call(
        functools.partial(add_kernel, begin),
        out_shape=jax.ShapeDtypeStruct(x.shape, BF),
        in_specs=[vm, vm],
        out_specs=vm,
        compiler_params=pltpu.CompilerParams(vmem_limit_bytes=VMEM_LIMIT),
        cost_estimate=cost(flops, 6 * x.size),
    )(x, y)


def after_kernel(x_ref, y_ref, after_ref, out_ref):
    out_ref[...] = (x_ref[...].astype(F32) + y_ref[...].astype(F32)).astype(BF)


def after_add(x, y, after):
    return pl.pallas_call(
        after_kernel,
        out_shape=jax.ShapeDtypeStruct(x.shape, BF),
        in_specs=[vm, vm, pl.BlockSpec(memory_space=pl.ANY)],
        out_specs=vm,
        compiler_params=pltpu.CompilerParams(vmem_limit_bytes=VMEM_LIMIT),
        cost_estimate=cost(x.size, 6 * x.size),
    )(x, y, after)


def body(three_index, occ_coef, pao_coef, ao_map, aux_map, ao_list):
    doms, ring = lax.axis_size("dom"), lax.axis_size("ao")
    aux_rows, mu_rows, nu_local = three_index.shape
    blocks = ao_list.shape[0]
    pao_d = pao_coef.shape[2]
    slab = three_index.reshape(aux_rows * mu_rows, nu_local)

    own = first_term(occ_coef, slab, ring)
    w = pick_rest(occ_coef, ring)
    slab, own = lax.optimization_barrier((slab, own))
    other_slab = swap(slab, doms)
    other = None
    half_ring = ring // 2
    for i in range(half_ring):
        if i == 0:
            other = term(w, i, other_slab)
        own = [hop(v, doms, ring) for v in own]
        if i == 0:
            own = [after_add(t, v, o) for t, v, o in zip(term(w, i, slab), own, other)]
        else:
            own = [add(t, v) for t, v in zip(term(w, i, slab), own)]
        if i < half_ring - 1:
            if i > 0:
                other = [steer_add(t, v, HINT_B) for t, v in zip(term(w, i, other_slab), other)]
            other = [hop(v, doms, ring, 1 if i == half_ring - 2 else 0) for v in other]
    halves = [add(v, o) for v, o in zip(own, other)]

    shells = pao_coef[0].reshape(-1, AOB, pao_d)
    keep = ao_map[0].astype(BF)[ao_list]
    projector = (shells[ao_list] * keep[:, :, None, None]).reshape(blocks, mu_rows, pao_d)
    half = jnp.stack([h.reshape(doms, OCC_D, aux_rows // PARTS, mu_rows) for h in halves], axis=2)
    half = half.reshape(doms, OCC_D, aux_rows, mu_rows)
    got = lax.all_to_all(half, "dom", split_axis=0, concat_axis=0, tiled=True)
    full = full_of(got, projector)
    near = lax.ppermute(full, "dom", [(d, (d + 1) % doms) for d in range(doms)])
    pair_self, turned = self_pair(full, aux_map)
    pair_near = near_pair(turned, near)
    return (pair_self, pair_near)


def solution(mesh):
    owner = P(("dom", "ao"), None, None)
    placed = (
        P("dom", None, "ao"),
        P("ao", None),
        owner,
        P(("dom", "ao"), None),
        P(("dom", "ao"), None),
        P(),
    )
    return jax.shard_map(body, mesh=mesh, in_specs=placed, out_specs=(owner, owner), check_vma=False)
```

```python
import functools

import jax
import jax.numpy as jnp
from jax import lax
from jax.experimental import pallas as pl
from jax.experimental.pallas import tpu as pltpu
from jax.sharding import PartitionSpec as P

QB = 128
AOB = 16
OCC_D = 2
vm = pl.BlockSpec(memory_space=pltpu.VMEM)
BF = jnp.bfloat16
F32 = jnp.float32
PARTS = 1
HINT_B = 1000000
FIRST_VMEM = 56 * 2**20
VMEM_LIMIT = 16 * 2**20


def hop(value, doms, ring, other=0):
    pairs = []
    for d in range(doms):
        step = 1 if d % 2 == 0 else -1
        for s in range(ring):
            pairs.append((d * ring + s, (d ^ other) * ring + (s + step) % ring))
    return lax.ppermute(value, ("dom", "ao"), pairs)


def swap(value, doms):
    return lax.ppermute(value, "dom", [(d, d ^ 1) for d in range(doms)])


def nt(x, y):
    return lax.dot_general(x, y, (((1,), (1,)), ((), ())), preferred_element_type=F32)


def pick_rows(occ, rows, ring, ahead):
    way = 1 - 2 * (lax.axis_index("dom") % 2)
    shard = (lax.axis_index("ao") + ahead * way + ring) % ring
    row = lax.broadcasted_iota(jnp.int32, (rows, occ.shape[1]), 0)
    col = lax.broadcasted_iota(jnp.int32, (rows, occ.shape[1]), 1)
    home = (row // OCC_D) * (ring * OCC_D) + row % OCC_D + shard * OCC_D
    pick = jnp.where(col == home, 1.0, 0.0).astype(BF)
    return nt(pick, occ).astype(BF)


def first_kernel(ring, occ_hbm, slab_hbm, *refs):
    out_refs = refs[:PARTS]
    occ_ref, slab_ref, occ_sem, slab_sems = refs[PARTS:]
    cut = slab_ref.shape[0] // PARTS
    occ_copy = pltpu.make_async_copy(occ_hbm, occ_ref, occ_sem)
    occ_copy.start()
    slab_copies = []
    for c in range(PARTS):
        part = pl.ds(c * cut, cut)
        slab_copies.append(pltpu.make_async_copy(slab_hbm.at[part], slab_ref.at[part], slab_sems.at[c]))
        slab_copies[-1].start()
    occ_copy.wait()
    w = pick_rows(occ_ref[...], out_refs[0].shape[0], ring, ring // 2)
    for c in range(PARTS):
        slab_copies[c].wait()
        out_refs[c][...] = nt(w, slab_ref[c * cut : (c + 1) * cut]).reshape(out_refs[c].shape).astype(BF)


def first_term(occ, slab, ring, aux_rows):
    rows, width = occ.shape[1] // ring, slab.shape[0] // PARTS
    vm, hbm = pl.BlockSpec(memory_space=pltpu.VMEM), pl.BlockSpec(memory_space=pl.ANY)
    return pl.pallas_call(
        functools.partial(first_kernel, ring),
        out_shape=[jax.ShapeDtypeStruct((rows, aux_rows // PARTS, width * PARTS // aux_rows), BF)] * PARTS,
        in_specs=[hbm, hbm],
        out_specs=[vm] * PARTS,
        scratch_shapes=[
            pltpu.VMEM(occ.shape, BF),
            pltpu.VMEM(slab.shape, BF),
            pltpu.SemaphoreType.DMA,
            pltpu.SemaphoreType.DMA((PARTS,)),
        ],
        compiler_params=pltpu.CompilerParams(vmem_limit_bytes=FIRST_VMEM),
        cost_estimate=pl.CostEstimate(flops=2 * rows * slab.size, bytes_accessed=3 << 20, transcendentals=0),
    )(occ, slab)


def pick_kernel(ring, occ_ref, w_ref):
    rows = occ_ref.shape[1] // ring
    for i in range(ring // 2):
        w_ref[i] = pick_rows(occ_ref[...], rows, ring, ring // 2 - 1 - i)


def pick_rest(occ, ring):
    rows = occ.shape[1] // ring
    return pl.pallas_call(
        functools.partial(pick_kernel, ring),
        out_shape=jax.ShapeDtypeStruct((ring // 2, rows, occ.shape[0]), BF),
        in_specs=[pl.BlockSpec(memory_space=pltpu.VMEM)],
        out_specs=pl.BlockSpec(memory_space=pltpu.VMEM),
        compiler_params=pltpu.CompilerParams(vmem_limit_bytes=VMEM_LIMIT),
        cost_estimate=pl.CostEstimate(flops=2 * (ring // 2) * rows * occ.size, bytes_accessed=2 << 20, transcendentals=0),
    )(occ)


def term_kernel(w_ref, slab_ref, *out_refs):
    cut = slab_ref.shape[0] // PARTS
    for c in range(PARTS):
        out_refs[c][...] = nt(w_ref[0], slab_ref[c * cut : (c + 1) * cut]).reshape(out_refs[c].shape).astype(BF)


def term(w, i, slab, aux_rows):
    rows, width = w.shape[1], slab.shape[0] // PARTS
    vm = pl.BlockSpec(memory_space=pltpu.VMEM)
    return pl.pallas_call(
        term_kernel,
        grid=(1,),
        out_shape=[jax.ShapeDtypeStruct((rows, aux_rows // PARTS, width * PARTS // aux_rows), BF)] * PARTS,
        in_specs=[pl.BlockSpec((1,) + w.shape[1:], lambda g: (i, 0, 0)), vm],
        out_specs=[vm] * PARTS,
        compiler_params=pltpu.CompilerParams(vmem_limit_bytes=VMEM_LIMIT),
        cost_estimate=pl.CostEstimate(flops=2 * rows * slab.size, bytes_accessed=3 << 20, transcendentals=0),
    )(w, slab)


def add(x, y):
    return (x.astype(F32) + y.astype(F32)).astype(BF)


def cost(flops, size):
    return pl.CostEstimate(flops=flops, bytes_accessed=size, transcendentals=0)


def full_kernel(got_ref, projector_ref, full_ref):
    doms, _, aux_rows, mu_rows = got_ref.shape
    blocks, _, pao_d = projector_ref.shape
    per = doms // blocks
    for b in range(blocks):
        part = got_ref[b * per : (b + 1) * per].astype(F32).reshape(per * OCC_D * aux_rows, mu_rows).astype(BF)
        t = jnp.dot(part, projector_ref[b], preferred_element_type=F32).reshape(per, OCC_D, aux_rows, pao_d)
        for k in range(OCC_D):
            rows = slice(b * per * aux_rows, (b + 1) * per * aux_rows)
            full_ref[rows, k * pao_d : (k + 1) * pao_d] = t[:, k].reshape(per * aux_rows, pao_d).astype(BF)


def full_of(got, projector):
    doms, _, aux_rows, _ = got.shape
    return pl.pallas_call(
        full_kernel,
        out_shape=jax.ShapeDtypeStruct((doms * aux_rows, OCC_D * projector.shape[2]), BF),
        in_specs=[vm, vm],
        out_specs=vm,
        compiler_params=pltpu.CompilerParams(vmem_limit_bytes=VMEM_LIMIT),
        cost_estimate=cost(2 * got.size * projector.shape[2], 1 << 20),
    )(got, projector)


def self_kernel(full_ref, keep_ref, out_ref, turned_ref):
    per = full_ref.shape[0] // keep_ref.shape[1]
    for b in range(keep_ref.shape[1]):
        rows = slice(b * per, (b + 1) * per)
        kept = full_ref[rows].astype(F32) * keep_ref[0, b].astype(F32)
        turned_ref[:, rows] = kept.T.astype(BF)
    out_ref[0] = jnp.dot(turned_ref[...], full_ref[...], preferred_element_type=F32).astype(BF)


def self_pair(full, aux_map):
    rows, width = full.shape
    return pl.pallas_call(
        self_kernel,
        out_shape=[jax.ShapeDtypeStruct((1, width, width), BF), jax.ShapeDtypeStruct((width, rows), BF)],
        in_specs=[vm, pl.BlockSpec(memory_space=pltpu.SMEM)],
        out_specs=[vm, vm],
        compiler_params=pltpu.CompilerParams(vmem_limit_bytes=VMEM_LIMIT),
        cost_estimate=cost(2 * rows * width * width, 1 << 20),
    )(full, aux_map)


def near_kernel(turned_ref, near_ref, out_ref):
    out_ref[0] = jnp.dot(turned_ref[...], near_ref[...], preferred_element_type=F32).astype(BF)


def near_pair(turned, near):
    rows, width = near.shape
    return pl.pallas_call(
        near_kernel,
        out_shape=jax.ShapeDtypeStruct((1, width, width), BF),
        in_specs=[vm, vm],
        out_specs=vm,
        compiler_params=pltpu.CompilerParams(vmem_limit_bytes=VMEM_LIMIT),
        cost_estimate=cost(2 * rows * width * width, 1 << 20),
    )(turned, near)


def add_kernel(x_ref, y_ref, out_ref):
    out_ref[...] = (x_ref[...].astype(F32) + y_ref[...].astype(F32)).astype(BF)


def steer_add(x, y, flops):
    return pl.pallas_call(
        add_kernel,
        out_shape=jax.ShapeDtypeStruct(x.shape, BF),
        in_specs=[vm, vm],
        out_specs=vm,
        compiler_params=pltpu.CompilerParams(vmem_limit_bytes=VMEM_LIMIT),
        cost_estimate=cost(flops, 6 * x.size),
    )(x, y)


def after_kernel(x_ref, y_ref, after_ref, out_ref):
    out_ref[...] = (x_ref[...].astype(F32) + y_ref[...].astype(F32)).astype(BF)


def after_add(x, y, after):
    return pl.pallas_call(
        after_kernel,
        out_shape=jax.ShapeDtypeStruct(x.shape, BF),
        in_specs=[vm, vm, pl.BlockSpec(memory_space=pl.ANY)],
        out_specs=vm,
        compiler_params=pltpu.CompilerParams(vmem_limit_bytes=VMEM_LIMIT),
        cost_estimate=cost(x.size, 6 * x.size),
    )(x, y, after)


def body(three_index, occ_coef, pao_coef, ao_map, aux_map, ao_list):
    doms, ring = lax.axis_size("dom"), lax.axis_size("ao")
    aux_rows, mu_rows, nu_local = three_index.shape
    blocks = ao_list.shape[0]
    pao_d = pao_coef.shape[2]
    slab = three_index.reshape(aux_rows * mu_rows, nu_local)

    own = first_term(occ_coef, slab, ring, aux_rows)
    w = pick_rest(occ_coef, ring)
    slab, own = lax.optimization_barrier((slab, own))
    other_slab = swap(slab, doms)
    other = None
    half_ring = ring // 2
    for i in range(half_ring):
        if i == 0:
            other = term(w, i, other_slab, aux_rows)
        own = [hop(v, doms, ring) for v in own]
        if i == 0:
            own = [after_add(t, v, o) for t, v, o in zip(term(w, i, slab, aux_rows), own, other)]
        else:
            own = [add(t, v) for t, v in zip(term(w, i, slab, aux_rows), own)]
        if i < half_ring - 1:
            if i > 0:
                other = [steer_add(t, v, HINT_B) for t, v in zip(term(w, i, other_slab, aux_rows), other)]
            other = [hop(v, doms, ring, 1 if i == half_ring - 2 else 0) for v in other]
    halves = [add(v, o) for v, o in zip(own, other)]

    shells = pao_coef[0].reshape(-1, AOB, pao_d)
    keep = ao_map[0].astype(BF)[ao_list]
    projector = (shells[ao_list] * keep[:, :, None, None]).reshape(blocks, mu_rows, pao_d)
    half = jnp.stack([h.reshape(doms, OCC_D, aux_rows // PARTS, mu_rows) for h in halves], axis=2)
    half = half.reshape(doms, OCC_D, aux_rows, mu_rows)
    got = lax.all_to_all(half, "dom", split_axis=0, concat_axis=0, tiled=True)
    full = full_of(got, projector)
    near = lax.ppermute(full, "dom", [(d, (d + 1) % doms) for d in range(doms)])
    pair_self, turned = self_pair(full, aux_map)
    pair_near = near_pair(turned, near)
    return (pair_self, pair_near)


def solution(mesh):
    owner = P(("dom", "ao"), None, None)
    placed = (
        P("dom", None, "ao"),
        P("ao", None),
        owner,
        P(("dom", "ao"), None),
        P(("dom", "ao"), None),
        P(),
    )
    return jax.shard_map(body, mesh=mesh, in_specs=placed, out_specs=(owner, owner), check_vma=False)
```

```python
import functools

import jax
import jax.numpy as jnp
from jax import lax
from jax.experimental import pallas as pl
from jax.experimental.pallas import tpu as pltpu
from jax.sharding import PartitionSpec as P

QB = 128
AOB = 16
OCC_D = 2
vm = pl.BlockSpec(memory_space=pltpu.VMEM)
BF = jnp.bfloat16
F32 = jnp.float32
PARTS = 1
HINT_B = 1000000
FIRST_VMEM = 56 * 2**20
VMEM_LIMIT = 16 * 2**20


def hop(value, doms, ring, other=0):
    pairs = []
    for d in range(doms):
        step = 1 if d % 2 == 0 else -1
        for s in range(ring):
            pairs.append((d * ring + s, (d ^ other) * ring + (s + step) % ring))
    return lax.ppermute(value, ("dom", "ao"), pairs)


def swap(value, doms):
    return lax.ppermute(value, "dom", [(d, d ^ 1) for d in range(doms)])


def nt(x, y):
    return lax.dot_general(x, y, (((1,), (1,)), ((), ())), preferred_element_type=F32)


def pick_rows(occ, rows, ring, ahead):
    way = 1 - 2 * (lax.axis_index("dom") % 2)
    shard = (lax.axis_index("ao") + ahead * way + ring) % ring
    row = lax.broadcasted_iota(jnp.int32, (rows, occ.shape[1]), 0)
    col = lax.broadcasted_iota(jnp.int32, (rows, occ.shape[1]), 1)
    home = (row // OCC_D) * (ring * OCC_D) + row % OCC_D + shard * OCC_D
    pick = jnp.where(col == home, 1.0, 0.0).astype(BF)
    return nt(pick, occ).astype(BF)


def first_kernel(ring, occ_hbm, slab_hbm, *refs):
    out_refs = refs[:PARTS]
    occ_ref, slab_ref, occ_sem, slab_sems = refs[PARTS:]
    cut = slab_ref.shape[0] // PARTS
    occ_copy = pltpu.make_async_copy(occ_hbm, occ_ref, occ_sem)
    occ_copy.start()
    slab_copies = []
    for c in range(PARTS):
        part = pl.ds(c * cut, cut)
        slab_copies.append(pltpu.make_async_copy(slab_hbm.at[part], slab_ref.at[part], slab_sems.at[c]))
        slab_copies[-1].start()
    occ_copy.wait()
    w = pick_rows(occ_ref[...], out_refs[0].shape[0], ring, ring // 2)
    for c in range(PARTS):
        slab_copies[c].wait()
        out_refs[c][...] = nt(w, slab_ref[c * cut : (c + 1) * cut]).reshape(out_refs[c].shape).astype(BF)


def first_term(occ, slab, ring, aux_rows):
    rows, width = occ.shape[1] // ring, slab.shape[0] // PARTS
    vm, hbm = pl.BlockSpec(memory_space=pltpu.VMEM), pl.BlockSpec(memory_space=pl.ANY)
    return pl.pallas_call(
        functools.partial(first_kernel, ring),
        out_shape=[jax.ShapeDtypeStruct((rows, aux_rows // PARTS, width * PARTS // aux_rows), BF)] * PARTS,
        in_specs=[hbm, hbm],
        out_specs=[vm] * PARTS,
        scratch_shapes=[
            pltpu.VMEM(occ.shape, BF),
            pltpu.VMEM(slab.shape, BF),
            pltpu.SemaphoreType.DMA,
            pltpu.SemaphoreType.DMA((PARTS,)),
        ],
        compiler_params=pltpu.CompilerParams(vmem_limit_bytes=FIRST_VMEM),
        cost_estimate=pl.CostEstimate(flops=2 * rows * slab.size, bytes_accessed=3 << 20, transcendentals=0),
    )(occ, slab)


def pick_kernel(ring, occ_ref, w_ref):
    rows = occ_ref.shape[1] // ring
    for i in range(ring // 2):
        w_ref[i] = pick_rows(occ_ref[...], rows, ring, ring // 2 - 1 - i)


def pick_rest(occ, ring):
    rows = occ.shape[1] // ring
    return pl.pallas_call(
        functools.partial(pick_kernel, ring),
        out_shape=jax.ShapeDtypeStruct((ring // 2, rows, occ.shape[0]), BF),
        in_specs=[pl.BlockSpec(memory_space=pltpu.VMEM)],
        out_specs=pl.BlockSpec(memory_space=pltpu.VMEM),
        compiler_params=pltpu.CompilerParams(vmem_limit_bytes=VMEM_LIMIT),
        cost_estimate=pl.CostEstimate(flops=2 * (ring // 2) * rows * occ.size, bytes_accessed=2 << 20, transcendentals=0),
    )(occ)


def term_kernel(w_ref, slab_ref, *out_refs):
    cut = slab_ref.shape[0] // PARTS
    for c in range(PARTS):
        out_refs[c][...] = nt(w_ref[0], slab_ref[c * cut : (c + 1) * cut]).reshape(out_refs[c].shape).astype(BF)


def term(w, i, slab, aux_rows):
    rows, width = w.shape[1], slab.shape[0] // PARTS
    vm = pl.BlockSpec(memory_space=pltpu.VMEM)
    return pl.pallas_call(
        term_kernel,
        grid=(1,),
        out_shape=[jax.ShapeDtypeStruct((rows, aux_rows // PARTS, width * PARTS // aux_rows), BF)] * PARTS,
        in_specs=[pl.BlockSpec((1,) + w.shape[1:], lambda g: (i, 0, 0)), vm],
        out_specs=[vm] * PARTS,
        compiler_params=pltpu.CompilerParams(vmem_limit_bytes=VMEM_LIMIT),
        cost_estimate=pl.CostEstimate(flops=2 * rows * slab.size, bytes_accessed=3 << 20, transcendentals=0),
    )(w, slab)


def add(x, y):
    return (x.astype(F32) + y.astype(F32)).astype(BF)


def cost(flops, size):
    return pl.CostEstimate(flops=flops, bytes_accessed=size, transcendentals=0)


def full_kernel(got_ref, projector_ref, full_ref):
    doms, _, aux_rows, mu_rows = got_ref.shape
    blocks, _, pao_d = projector_ref.shape
    per = doms // blocks
    for b in range(blocks):
        part = got_ref[b * per : (b + 1) * per].astype(F32).reshape(per * OCC_D * aux_rows, mu_rows).astype(BF)
        t = jnp.dot(part, projector_ref[b], preferred_element_type=F32).reshape(per, OCC_D, aux_rows, pao_d)
        for k in range(OCC_D):
            rows = slice(b * per * aux_rows, (b + 1) * per * aux_rows)
            full_ref[rows, k * pao_d : (k + 1) * pao_d] = t[:, k].reshape(per * aux_rows, pao_d).astype(BF)


def full_of(got, projector):
    doms, _, aux_rows, _ = got.shape
    return pl.pallas_call(
        full_kernel,
        out_shape=jax.ShapeDtypeStruct((doms * aux_rows, OCC_D * projector.shape[2]), BF),
        in_specs=[vm, vm],
        out_specs=vm,
        compiler_params=pltpu.CompilerParams(vmem_limit_bytes=VMEM_LIMIT),
        cost_estimate=cost(2 * got.size * projector.shape[2], 1 << 20),
    )(got, projector)


def self_kernel(full_ref, keep_ref, out_ref, turned_ref):
    per = full_ref.shape[0] // keep_ref.shape[1]
    for b in range(keep_ref.shape[1]):
        rows = slice(b * per, (b + 1) * per)
        kept = full_ref[rows].astype(F32) * keep_ref[0, b].astype(F32)
        turned_ref[:, rows] = kept.T.astype(BF)
    out_ref[0] = jnp.dot(turned_ref[...], full_ref[...], preferred_element_type=F32).astype(BF)


def self_pair(full, aux_map):
    rows, width = full.shape
    return pl.pallas_call(
        self_kernel,
        out_shape=[jax.ShapeDtypeStruct((1, width, width), BF), jax.ShapeDtypeStruct((width, rows), BF)],
        in_specs=[vm, pl.BlockSpec(memory_space=pltpu.SMEM)],
        out_specs=[vm, vm],
        compiler_params=pltpu.CompilerParams(vmem_limit_bytes=VMEM_LIMIT),
        cost_estimate=cost(2 * rows * width * width, 1 << 20),
    )(full, aux_map)


def near_kernel(turned_ref, near_ref, out_ref):
    out_ref[0] = jnp.dot(turned_ref[...], near_ref[...], preferred_element_type=F32).astype(BF)


def near_pair(turned, near):
    rows, width = near.shape
    return pl.pallas_call(
        near_kernel,
        out_shape=jax.ShapeDtypeStruct((1, width, width), BF),
        in_specs=[vm, vm],
        out_specs=vm,
        compiler_params=pltpu.CompilerParams(vmem_limit_bytes=VMEM_LIMIT),
        cost_estimate=cost(2 * rows * width * width, 1 << 20),
    )(turned, near)


def add_kernel(x_ref, y_ref, out_ref):
    out_ref[...] = (x_ref[...].astype(F32) + y_ref[...].astype(F32)).astype(BF)


def steer_add(x, y, flops):
    return pl.pallas_call(
        add_kernel,
        out_shape=jax.ShapeDtypeStruct(x.shape, BF),
        in_specs=[vm, vm],
        out_specs=vm,
        compiler_params=pltpu.CompilerParams(vmem_limit_bytes=VMEM_LIMIT),
        cost_estimate=cost(flops, 6 * x.size),
    )(x, y)


def after_kernel(x_ref, y_ref, after_ref, out_ref):
    out_ref[...] = (x_ref[...].astype(F32) + y_ref[...].astype(F32)).astype(BF)


def after_add(x, y, after):
    return pl.pallas_call(
        after_kernel,
        out_shape=jax.ShapeDtypeStruct(x.shape, BF),
        in_specs=[vm, vm, pl.BlockSpec(memory_space=pl.ANY)],
        out_specs=vm,
        compiler_params=pltpu.CompilerParams(vmem_limit_bytes=VMEM_LIMIT),
        cost_estimate=cost(x.size, 6 * x.size),
    )(x, y, after)


def body(three_index, occ_coef, pao_coef, ao_map, aux_map, ao_list):
    doms, ring = lax.axis_size("dom"), lax.axis_size("ao")
    aux_rows, mu_rows, nu_local = three_index.shape
    blocks = ao_list.shape[0]
    pao_d = pao_coef.shape[2]
    slab = three_index.reshape(aux_rows * mu_rows, nu_local)

    own = first_term(occ_coef, slab, ring, aux_rows)
    w = pick_rest(occ_coef, ring)
    slab, own = lax.optimization_barrier((slab, own))
    other_slab = swap(slab, doms)
    other = None
    half_ring = ring // 2
    for i in range(half_ring):
        if i == 0:
            other = term(w, i, other_slab, aux_rows)
        own = [hop(v, doms, ring) for v in own]
        if i == 0:
            own = [after_add(t, v, o) for t, v, o in zip(term(w, i, slab, aux_rows), own, other)]
        elif i < half_ring - 1:
            own = [add(t, v) for t, v in zip(term(w, i, slab, aux_rows), own)]
        if i < half_ring - 1:
            if i > 0:
                other = [steer_add(t, v, HINT_B) for t, v in zip(term(w, i, other_slab, aux_rows), other)]
            other = [hop(v, doms, ring, 1 if i == half_ring - 2 else 0) for v in other]
    other = [steer_add(t, o, HINT_B) for t, o in zip(term(w, half_ring - 1, slab, aux_rows), other)]
    halves = [add(v, o) for v, o in zip(own, other)]

    shells = pao_coef[0].reshape(-1, AOB, pao_d)
    keep = ao_map[0].astype(BF)[ao_list]
    projector = (shells[ao_list] * keep[:, :, None, None]).reshape(blocks, mu_rows, pao_d)
    half = jnp.stack([h.reshape(doms, OCC_D, aux_rows // PARTS, mu_rows) for h in halves], axis=2)
    half = half.reshape(doms, OCC_D, aux_rows, mu_rows)
    got = lax.all_to_all(half, "dom", split_axis=0, concat_axis=0, tiled=True)
    full = full_of(got, projector)
    near = lax.ppermute(full, "dom", [(d, (d + 1) % doms) for d in range(doms)])
    pair_self, turned = self_pair(full, aux_map)
    pair_near = near_pair(turned, near)
    return (pair_self, pair_near)


def solution(mesh):
    owner = P(("dom", "ao"), None, None)
    placed = (
        P("dom", None, "ao"),
        P("ao", None),
        owner,
        P(("dom", "ao"), None),
        P(("dom", "ao"), None),
        P(),
    )
    return jax.shard_map(body, mesh=mesh, in_specs=placed, out_specs=(owner, owner), check_vma=False)
```
